512 devices in a mesh: seq: 128 (over z, y, core), mp: 4 (over x).
Axes of the slice: x: 4, y: 8, z: 8, core: 2. Of those that a mesh axis runs over, the one named last changes fastest.
Arguments:
- x_in: bfloat16 [16384, 8192], P('seq', 'mp'), may hold values from -6 to 6
- bc_in: bfloat16 [16384, 2, 1024], P('seq', None, 'mp'), may hold values from -4 to 4
- dt_raw: bfloat16 [16384, 128], P('seq', 'mp'), may hold values from -4 to 4
- doc_id: int32 [16384], P('seq'), may hold values from 0 to 4, as said below
- conv_x: float32 [4, 8192], P(None, 'mp'), may hold values from -3 to 3
- bias_x: float32 [8192], P('mp'), may hold values from -3 to 3
- conv_bc: float32 [4, 2, 1024], P(None, None, 'mp'), may hold values from -3 to 3
- bias_bc: float32 [2, 1024], P(None, 'mp'), may hold values from -3 to 3
- rate: float32 [128], P('mp'), may hold values from 2e-05 to 0.1
- dskip: float32 [128], P('mp'), may hold values from 0.5 to 4
- z_in: bfloat16 [16384, 8192], P('seq', 'mp'), may hold values from -6 to 6
- norm_gain: float32 [8192], P('mp'), may hold values from 0.1 to 1.9
Outputs:
- mixed: bfloat16 [16384, 8192], P('seq', 'mp')
The draws below stay inside these ranges and needn't reach their ends.
Inputs may be any that keep to these rules, and one draw needn't show every extreme that they name: doc_id of storage row i names the document of position p(i); along positions it starts at 0 and rises by 0 or 1 from one position to the next; the window holds 5 documents.
All inputs are finite; a program needn't handle non-finite values.
Results may differ from the reference program's by a relative error of at most 0.009.
Values may be sent and summed in bfloat16 or wider, within the bound.
A program may use at most 64 MiB of HBM per device.

```python
import math
import jax
import jax.numpy as jnp
from jax import lax

HEADS = 128
HDIM = 64
DSTATE = 128
GROUPS = 8
KCONV = 4
SPAN = 256
TOK_DEV = 128
DI = 8192
GDS = 1024
TOKENS = 16384
DOCS = 5
RUNS = 16
RUN = 8
N_SEQ = 128


def draw_doc_id(key, part):
    order = jax.random.permutation(key, TOKENS - 1) + 1
    chosen = order[:DOCS - 1]
    starts = jnp.zeros((TOKENS,), jnp.int32).at[0].set(1)
    starts = starts.at[chosen].set(1)
    documents = jnp.cumsum(starts) - 1
    return documents.reshape(RUNS, N_SEQ, RUN).swapaxes(0, 1).reshape(TOKENS).astype(jnp.int32)


def block_scale(own_key, shape, cuts, least, top_value):
    def one(axis_at, shards_of):
        heights = jax.random.uniform(jax.random.fold_in(jax.random.fold_in(own_key, 6), axis_at), (shards_of,), jnp.float32, least / len(cuts), top_value / len(cuts))
        return jnp.repeat(jnp.exp(heights), shape[axis_at] // shards_of).reshape((-1,) + (1,) * (len(shape) - axis_at - 1))

    level = one(*cuts[0])
    for cut in cuts[1:]:
        level = level * one(*cut)
    return level


def noise(rng, dims, scale, reach, pieces=(), kind=jnp.bfloat16):
    gain = block_scale(rng, dims, pieces, -0.22, 0.18) if pieces else 1.0
    drawn = jax.random.normal(rng, dims, jnp.float32) * scale * gain
    return jnp.minimum(jnp.maximum(drawn, -reach), reach).astype(kind)


def setup_inputs(seed: int = 0) -> dict:
    seeds = jax.random.split(jax.random.key(seed), 13)
    x_in = noise(seeds[0], (TOKENS, DI), 1.0, 6.0, ((0, 128), (1, 4)))
    bc_in = noise(seeds[1], (TOKENS, 2, GDS), 0.3, 4.0, ((0, 128), (2, 4)))
    dt_raw = noise(seeds[2], (TOKENS, HEADS), 1.0, 4.0, ((0, 128), (1, 4)))
    doc_id = draw_doc_id(jax.random.fold_in(seeds[12], 71), 0)
    conv_x = noise(seeds[4], (KCONV, DI), KCONV ** -0.5, 3.0, ((1, 4),), jnp.float32)
    bias_x = noise(seeds[5], (DI,), 0.3, 3.0, ((0, 4),), jnp.float32)
    conv_bc = noise(seeds[6], (KCONV, 2, GDS), KCONV ** -0.5, 3.0, ((2, 4),), jnp.float32)
    bias_bc = noise(seeds[7], (2, GDS), 0.3, 3.0, ((1, 4),), jnp.float32)
    rate = jnp.clip(jnp.exp(math.log(0.1) - 8.517193 * jax.random.uniform(seeds[8], (HEADS,), jnp.float32) ** block_scale(seeds[8], (HEADS,), ((0, 4),), -0.2, 0.2)), 1.9999999494757503e-05, 0.1)
    dskip = jnp.clip(jnp.exp(math.log(4.0) - 2.0794415 * jax.random.uniform(seeds[9], (HEADS,), jnp.float32) ** block_scale(seeds[9], (HEADS,), ((0, 4),), -0.2, 0.2)), 0.5, 4.0)
    z_in = noise(seeds[10], (TOKENS, DI), 1.0, 6.0, ((0, 128), (1, 4)))
    norm_gain = jnp.clip(1.0 + 0.18 * jax.random.normal(seeds[11], (DI,), jnp.float32), 0.1, 1.9)
    return {"x_in": x_in, "bc_in": bc_in, "dt_raw": dt_raw, "doc_id": doc_id, "conv_x": conv_x, "bias_x": bias_x, "conv_bc": conv_bc, "bias_bc": bias_bc, "rate": rate, "dskip": dskip, "z_in": z_in, "norm_gain": norm_gain}


EPSILON = 1e-05

def conv_runs(extended, extended_docs, weight, bias, tap_count):
    row_count = extended.shape[1] - tap_count + 1
    own_docs = extended_docs[:, tap_count - 1:]
    total = jnp.zeros((extended.shape[0], row_count, extended.shape[2]), jnp.float32) + bias
    for offset in range(tap_count):
        same_doc = (extended_docs[:, offset:offset + row_count] == own_docs).astype(jnp.float32)[:, :, None]
        total = total + weight[offset] * extended[:, offset:offset + row_count].astype(jnp.float32) * same_doc
    return jax.nn.silu(total).astype(jnp.bfloat16)

def span_terms(x_spans, b_spans, c_spans, step_size, head_rate, span_docs):
    size = span_docs.shape[1]
    decay_sum = jnp.cumsum(-step_size * head_rate, axis=1)
    scores = jnp.einsum('cin,cjn->cij', c_spans, b_spans, preferred_element_type=jnp.float32)
    row_index = lax.broadcasted_iota(jnp.int32, (size, size), 0)
    col_index = lax.broadcasted_iota(jnp.int32, (size, size), 1)
    visible = (span_docs[:, :, None] == span_docs[:, None, :]) & (row_index >= col_index)
    visible = visible[..., None]
    spread = jnp.where(visible, decay_sum[:, :, None, :] - decay_sum[:, None, :, :], 0.0)
    mixing = jnp.where(visible, scores[..., None] * jnp.exp(spread) * step_size[:, None, :, :], 0.0).astype(jnp.bfloat16)
    inner = jnp.einsum('cijh,cjhp->cihp', mixing, x_spans, preferred_element_type=jnp.float32)
    last_doc = span_docs[:, -1:]
    tail_weight = jnp.exp(decay_sum[:, -1:, :] - decay_sum) * step_size * (span_docs == last_doc).astype(jnp.float32)[:, :, None]
    weighted = (b_spans.astype(jnp.float32)[:, :, None, :] * tail_weight[..., None]).astype(jnp.bfloat16)
    states = jnp.einsum('cjhn,cjhp->chnp', weighted, x_spans, preferred_element_type=jnp.float32)
    through = jnp.exp(decay_sum[:, -1, :]) * (span_docs[:, :1] == last_doc).astype(jnp.float32)
    return (inner, decay_sum, (states, through, span_docs[:, :1], last_doc))

def outputs(x_spans, c_spans, head_skip, inner, decay_sum, span_docs, incoming, incoming_doc):
    cross = jnp.einsum('cin,chnp->cihp', c_spans, incoming.astype(jnp.bfloat16), preferred_element_type=jnp.float32)
    scale = jnp.exp(decay_sum) * (span_docs == incoming_doc[:, None]).astype(jnp.float32)[:, :, None]
    return inner + cross * scale[..., None] + head_skip[:, None] * x_spans.astype(jnp.float32)

def reference(x_in, bc_in, dt_raw, doc_id, conv_x, bias_x, conv_bc, bias_bc, rate, dskip, z_in, norm_gain):

    def to_sequence(array):
        return array.reshape((N_SEQ, RUNS, RUN) + array.shape[1:]).swapaxes(0, 1).reshape((TOKENS,) + array.shape[1:])

    def to_storage(array):
        return array.reshape((RUNS, N_SEQ, RUN) + array.shape[1:]).swapaxes(0, 1).reshape((TOKENS,) + array.shape[1:])
    margin = KCONV - 1
    group_heads = HEADS // GROUPS
    group_width = group_heads * HDIM
    span_count = TOKENS // SPAN
    docs = to_sequence(doc_id)
    extended_docs = jnp.concatenate([jnp.full((margin,), -1, jnp.int32), docs])[None]
    x_sequence = to_sequence(x_in)
    bc_sequence = to_sequence(bc_in)
    dt_sequence = to_sequence(dt_raw)

    def one_group(group):
        x_part = lax.dynamic_slice_in_dim(x_sequence, group * group_width, group_width, 1)
        bc_part = lax.dynamic_slice_in_dim(bc_sequence, group * DSTATE, DSTATE, 2).reshape(TOKENS, 2 * DSTATE)
        x_taps = lax.dynamic_slice_in_dim(conv_x, group * group_width, group_width, 1)
        x_bias = lax.dynamic_slice_in_dim(bias_x, group * group_width, group_width, 0)
        bc_taps = lax.dynamic_slice_in_dim(conv_bc, group * DSTATE, DSTATE, 2).reshape(KCONV, 2 * DSTATE)
        bc_bias = lax.dynamic_slice_in_dim(bias_bc, group * DSTATE, DSTATE, 1).reshape(2 * DSTATE)
        x_conv = conv_runs(jnp.concatenate([jnp.zeros((margin, group_width), x_part.dtype), x_part])[None], extended_docs, x_taps, x_bias, KCONV)[0]
        bc_conv = conv_runs(jnp.concatenate([jnp.zeros((margin, 2 * DSTATE), bc_part.dtype), bc_part])[None], extended_docs, bc_taps, bc_bias, KCONV)[0]
        step_size = jax.nn.softplus(lax.dynamic_slice_in_dim(dt_sequence, group * group_heads, group_heads, 1).astype(jnp.float32))
        head_rate = lax.dynamic_slice_in_dim(rate, group * group_heads, group_heads, 0)
        head_skip = lax.dynamic_slice_in_dim(dskip, group * group_heads, group_heads, 0)
        items = (x_conv.reshape(span_count, 1, SPAN, group_heads, HDIM), bc_conv[:, :DSTATE].reshape(span_count, 1, SPAN, DSTATE), bc_conv[:, DSTATE:].reshape(span_count, 1, SPAN, DSTATE), step_size.reshape(span_count, 1, SPAN, group_heads), docs.reshape(span_count, 1, SPAN))

        def advance(carried, item):
            state, before = carried
            x_spans, b_spans, c_spans, steps, span_docs = item
            inner, decay_sum, summary = span_terms(x_spans, b_spans, c_spans, steps, head_rate, span_docs)
            out_rows = outputs(x_spans, c_spans, head_skip, inner, decay_sum, span_docs, state[None], before)
            passed = summary[1][0] * (before == summary[2][0]).astype(jnp.float32)
            new_state = summary[0][0] + passed[:, None, None] * state
            return ((new_state, summary[3][0]), out_rows[0].astype(jnp.bfloat16))
        start = (jnp.zeros((group_heads, DSTATE, HDIM), jnp.float32), jnp.full((1,), -1, jnp.int32))
        produced = lax.scan(advance, start, items)[1]
        return produced.reshape(TOKENS, group_width)
    per_group = lax.map(one_group, jnp.arange(GROUPS))
    y_storage = to_storage(jnp.moveaxis(per_group, 0, 1).reshape(TOKENS, DI))

    def norm_block(pair):
        y_block, z_block = pair
        gated = y_block.astype(jnp.float32) * jax.nn.silu(z_block.astype(jnp.float32))
        square = lax.optimization_barrier(jnp.sum(gated * gated, axis=1))
        return (gated * lax.rsqrt(square / DI + EPSILON)[:, None] * norm_gain).astype(jnp.bfloat16)
    mixed = lax.map(norm_block, (y_storage.reshape(N_SEQ, TOK_DEV, DI), z_in.reshape(N_SEQ, TOK_DEV, DI)))
    return mixed.reshape(TOKENS, DI)
```

```python
import jax
import jax.numpy as jnp
from jax import lax
from jax.experimental import pallas as pl
from jax.experimental.pallas import tpu as pltpu
from jax.sharding import PartitionSpec as P

MESH = pl.DeviceIdType.MESH
F32 = jnp.float32
BF16 = jnp.bfloat16

DSTATE = 128
HDIM = 64
SPAN = 256
DI = 8192
EPSILON = 1e-05

RUNS = 16
RUN = 8
HALF = 64
SEGS = 32
SEG = 512
PIECES = 4
WIDTH = 512
LOCAL = 2048
AUX = 384
SLICE = 16


def split(value, parts):
    out = []
    for _ in range(parts):
        piece = value.astype(BF16)
        out.append(piece)
        value = value - piece.astype(F32)
    return jnp.concatenate(out, axis=1)


def dot(a, b, dims=((1,), (0,))):
    return lax.dot_general(a, b, (dims, ((), ())), preferred_element_type=F32)


def silu(u):
    return u * lax.logistic(u)


def body(
    x_hbm,
    aux_hbm,
    z_hbm,
    conv_x,
    bias_x,
    conv_bc,
    bias_bc,
    rate,
    dskip,
    gain,
    out_ref,
    xr,
    ar,
    ext,
    same,
    xc,
    bcc,
    xin,
    xst,
    eout,
    inner,
    srows,
    sbuf,
    srecv,
    inb,
    inr,
    ysend,
    yrecv,
    zbuf,
    part,
    send_sem,
    recv_x,
    recv_a,
    halo_sem,
    state_sem,
    back_sem,
    y_sem,
    part_sem,
    z_sem,
):
    me = lax.axis_index("seq")
    col = lax.axis_index("mp")
    n_col = lax.axis_size("mp")
    half = me // HALF
    t = me % HALF
    q = t // PIECES
    w = t % PIECES
    group = w // 2
    seg = q * 2 + half

    def remote(src, dst, sent, got, seq, mp=col):
        return pltpu.make_async_remote_copy(
            src_ref=src,
            dst_ref=dst,
            send_sem=sent,
            recv_sem=got,
            device_id=(seq, mp),
            device_id_type=MESH,
        )

    def seg_device(r):
        return (r % 2) * HALF + (r // 2) * PIECES + w

    def take(buf, sem):
        pltpu.make_async_copy(buf, buf, sem).wait()

    barrier = pltpu.get_barrier_semaphore()

    @pl.loop(0, HALF - 1)
    def _(k):
        pl.semaphore_signal(
            barrier, inc=1, device_id=(half * HALF + (t + 1 + k) % HALF, col), device_id_type=MESH
        )

    @pl.loop(0, RUNS)
    def _(k):
        pl.semaphore_signal(
            barrier,
            inc=1,
            device_id=((1 - half) * HALF + k * PIECES + w, col),
            device_id_type=MESH,
        )

    for k in range(1, n_col):
        pl.semaphore_signal(
            barrier, inc=1, device_id=(me, (col + k) % n_col), device_id_type=MESH
        )
    pl.semaphore_wait(barrier, HALF - 1 + RUNS + n_col - 1)

    kind = t // 32 + t // 63

    def x_block(d):
        return x_hbm.at[d // PIECES, :, pl.ds(pl.multiple_of((d % PIECES) * WIDTH, 128), WIDTH)]

    def aux_block(d):
        return aux_hbm.at[d // PIECES, (d % PIECES) // 2]

    @pl.loop(1, HALF)
    def _(k):
        d = (t + k) % HALF
        remote(
            aux_block(d), ar.at[1 + t], send_sem.at[1], recv_a.at[kind], half * HALF + d
        ).start()
        remote(x_block(d), xr.at[1 + t], send_sem.at[0], recv_x.at[kind], half * HALF + d).start()

    pltpu.make_async_copy(x_block(t), xr.at[1 + t], recv_x.at[kind]).start()
    pltpu.make_async_copy(aux_block(t), ar.at[1 + t], recv_a.at[kind]).start()
    z_copy = pltpu.make_async_copy(z_hbm, zbuf, z_sem)
    z_copy.start()

    following = seg_device((seg + 1) % SEGS)
    take(xr.at[pl.ds(64, 1)], recv_x.at[2])
    take(ar.at[pl.ds(64, 1)], recv_a.at[2])
    halo_x = remote(xr.at[64], xr.at[0], halo_sem.at[0], halo_sem.at[1], following)
    halo_a = remote(ar.at[64], ar.at[0], halo_sem.at[2], halo_sem.at[3], following)
    halo_x.start()
    halo_a.start()

    lane = lax.broadcasted_iota(jnp.int32, (128, WIDTH), 1)
    row = lax.broadcasted_iota(jnp.int32, (128, WIDTH), 0)
    spread = (row == w * 8 + lax.shift_right_logical(lane, 6)).astype(F32).astype(BF16)
    spread = jnp.concatenate([spread] * 3, axis=0)

    take(ar.at[pl.ds(1, 32)], recv_a.at[0])
    take(ar.at[pl.ds(33, 31)], recv_a.at[1])
    halo_a.wait()

    docs = ar[:, :, 256:384].astype(F32).reshape(SEG + 8, 128)
    docs = jnp.broadcast_to(docs[:, 127:128], (SEG + 8, 128))
    ahead = lax.broadcasted_iota(jnp.int32, (SEG + 8, 128), 0) < 8
    docs = jnp.where(jnp.logical_and(ahead, seg == 0), -1.0, docs)
    ext[...] = docs
    own = ext[8:, :]
    for k in range(1, 4):
        same[k - 1] = (ext[8 - k : 8 - k + SEG, :] == own).astype(F32)
    before = ext[7:8, :]
    last = ext[SEG + 7 : SEG + 8, :]
    from_before = (own == before).astype(F32)
    to_last = (own == last).astype(F32)
    marks = (own == lax.broadcasted_iota(jnp.int32, (SEG, 128), 1).astype(F32)).astype(F32)
    marks = marks.astype(BF16)
    kept = (before == last).astype(F32)

    def conv(block, taps, bias):
        ext[...] = block
        total = bias + taps[3:4] * ext[8:, :]
        for k in range(1, 4):
            total = total + taps[3 - k : 4 - k] * ext[8 - k : 8 - k + SEG, :] * same[k - 1]
        return silu(total).astype(BF16)

    for k in range(2):
        at = pl.ds(pl.multiple_of(k * 256 + group * 128, 128), 128)
        bcc[:, k * 128 : k * 128 + 128] = conv(
            ar[:, :, k * 128 : k * 128 + 128].astype(F32).reshape(SEG + 8, 128),
            conv_bc[:, at],
            bias_bc[:, at],
        )

    raw = ar[1:, :, 256:384].astype(F32).reshape(SEG, 128)
    step = jnp.maximum(raw, 0.0) + jnp.log1p(jnp.exp(-jnp.abs(raw)))
    log_decay = split(-step * rate[...], 3)
    tri = (
        lax.broadcasted_iota(jnp.int32, (SPAN, SPAN), 0)
        >= lax.broadcasted_iota(jnp.int32, (SPAN, SPAN), 1)
    ).astype(F32)
    tri_bf = tri.astype(BF16)
    mids, lasts = [], []
    for c in range(2):
        at = slice(c * SPAN, c * SPAN + SPAN)
        sums = dot(tri_bf, log_decay[at])
        decay = sums[:, :128] + sums[:, 128:256] + sums[:, 256:]
        mid, end = decay[127:128], decay[255:256]
        mids.append(mid)
        lasts.append(end)
        into = jnp.exp(mid - decay) * step[at]
        xin[at] = dot(split(into, 2), spread[:256])
        eout[at] = dot(split(jnp.exp(decay - mid), 2), spread[:256])
    rows = jnp.concatenate(
        [
            jnp.exp(mids[0]),
            jnp.exp(mids[1] + lasts[0] - mids[0]),
            jnp.exp(mids[1] + lasts[0]),
            jnp.exp(lasts[0] - mids[0] + lasts[1]),
            jnp.exp(lasts[1] - mids[1]),
            dskip[...],
            jnp.zeros((2, 128), F32),
        ],
        axis=0,
    )
    srows[...] = dot(split(rows, 3), spread)

    take(xr.at[pl.ds(1, 32)], recv_x.at[0])
    take(xr.at[pl.ds(33, 31)], recv_x.at[1])
    halo_x.wait()

    for j in range(4):
        at = slice(j * 128, j * 128 + 128)
        far = pl.ds(pl.multiple_of(w * WIDTH + j * 128, 128), 128)
        mixed = conv(
            xr[:, :, at].astype(F32).reshape(SEG + 8, 128), conv_x[:, far], bias_x[:, far]
        )
        xc[:, at] = mixed
        scaled = mixed.astype(F32) * xin[:, at]
        xst[:SPAN, at] = (scaled[:SPAN] * srows[3:4, at]).astype(BF16)
        xst[SPAN:, at] = (scaled[SPAN:] * srows[4:5, at]).astype(BF16)
        xin[:, at] = scaled

    weighted = (bcc[:, :128].astype(F32) * to_last).astype(BF16)
    state = dot(xst[...], weighted, ((0,), (0,)))
    passed = jnp.exp(lasts[0] + lasts[1]) * kept
    high = passed.astype(BF16).astype(F32)
    which = lax.broadcasted_iota(jnp.int32, (SLICE, 128), 0)
    tile = jnp.where(which == 0, high, jnp.where(which == 1, passed - high, 0.0))
    sbuf[:, :SLICE] = state.reshape(SEGS, SLICE, 128).astype(BF16)
    sbuf[:, SLICE:] = jnp.broadcast_to(tile.astype(BF16)[None], (SEGS, SLICE, 128))

    @pl.loop(1, SEGS)
    def _(k):
        r = (seg + k) % SEGS
        remote(sbuf.at[r], srecv.at[seg], send_sem.at[2], state_sem, seg_device(r)).start()

    pltpu.make_async_copy(sbuf.at[seg], srecv.at[seg], state_sem).start()

    for c in range(2):
        at = slice(c * SPAN, c * SPAN + SPAN)
        seen = dot(marks[at], marks[at], ((1,), (1,))) * tri
        scores = dot(bcc[at, 128:], bcc[at, :128], ((1,), (1,)))
        total = dot((scores * seen).astype(BF16), xin[at].astype(BF16))
        if c:
            seen = dot(marks[at], marks[:SPAN], ((1,), (1,)))
            scores = dot(bcc[at, 128:], bcc[:SPAN, :128], ((1,), (1,)))
            total = total + dot((scores * seen).astype(BF16), xin[:SPAN].astype(BF16)) * srows[1:2]
        inner[at] = total
    reads = (bcc[:, 128:].astype(F32) * from_before).astype(BF16)

    take(srecv, state_sem)
    head = lax.broadcasted_iota(jnp.int32, (SEGS, 128), 1) == w * 8 + seg // 4
    factor = srecv[:, SLICE : SLICE + 8, :].astype(F32)
    factor = jnp.sum(factor, axis=1)
    factor = jnp.sum(jnp.where(head, factor, 0.0), axis=1, keepdims=True)
    carried = jnp.zeros((SLICE, 128), F32)
    for g in range(SEGS):
        inb[g] = carried.astype(BF16)
        carried = srecv[g, :SLICE, :].astype(F32) + factor[g : g + 1] * carried

    @pl.loop(1, SEGS)
    def _(k):
        r = (seg + k) % SEGS
        remote(inb.at[r], inr.at[seg], send_sem.at[3], back_sem, seg_device(r)).start()

    pltpu.make_async_copy(inb.at[seg], inr.at[seg], back_sem).start()

    z_copy.wait()

    take(inr, back_sem)
    incoming = inr[...].reshape(SEG, 128)

    for c in range(2):
        at = slice(c * SPAN, c * SPAN + SPAN)
        cross = dot(reads[at], incoming, ((1,), (1,))) * srows[2 * c : 2 * c + 1]
        y = (inner[at] + cross) * eout[at] + srows[5:6] * xc[at].astype(F32)
        ysend[c * 32 : c * 32 + 32] = y.reshape(32, RUN, WIDTH).astype(BF16)
        place = yrecv.at[q, :, pl.ds(pl.multiple_of(w * WIDTH, 128), WIDTH)]

        @pl.loop(0, 32)
        def _(k):
            d = c * 32 + (t + k) % 32

            @pl.when(d != t)
            def _():
                remote(ysend.at[d], place, send_sem.at[4], y_sem, half * HALF + d).start()

    pltpu.make_async_copy(
        ysend.at[t], yrecv.at[q, :, pl.ds(pl.multiple_of(w * WIDTH, 128), WIDTH)], y_sem
    ).start()

    take(yrecv, y_sem)
    gated = yrecv[...].astype(F32).reshape(RUNS * RUN, LOCAL) * silu(
        zbuf[...].astype(F32).reshape(RUNS * RUN, LOCAL)
    )
    square = jnp.sum(gated * gated, axis=1, keepdims=True)
    part[col] = jnp.transpose(jnp.broadcast_to(square, (128, 128)))[:8]
    for k in range(1, n_col):
        remote(
            part.at[col], part.at[col], send_sem.at[5], part_sem, me, (col + k) % n_col
        ).start()
    take(part.at[pl.ds(0, n_col - 1)], part_sem)
    total = jnp.sum(part[...], axis=0)
    total = jnp.transpose(jnp.broadcast_to(total[:1], (128, 128)))[:, :1]
    out_ref[...] = (gated * lax.rsqrt(total / DI + EPSILON) * gain[...]).astype(BF16)

    take(xr.at[pl.ds(0, 63)], send_sem.at[0])
    take(ar.at[pl.ds(0, 63)], send_sem.at[1])
    take(sbuf.at[pl.ds(0, 31)], send_sem.at[2])
    take(inb.at[pl.ds(0, 31)], send_sem.at[3])
    take(ysend.at[pl.ds(0, 63)], send_sem.at[4])
    take(part.at[pl.ds(0, n_col - 1)], send_sem.at[5])


def local(
    x_in, bc_in, dt_raw, doc_id, conv_x, bias_x, conv_bc, bias_bc, rate, dskip, z_in, norm_gain
):
    n_col = lax.axis_size("mp")
    rows = x_in.shape[0]
    heads = rate.shape[0]
    bc = bc_in.reshape(RUNS, RUN, 2, 2, DSTATE).transpose(0, 3, 1, 2, 4)
    bc = bc.reshape(RUNS, 2, RUN, 2 * DSTATE)
    tail = jnp.concatenate(
        [dt_raw, jnp.broadcast_to(doc_id.astype(BF16)[:, None], (rows, 128 - heads))], axis=1
    )
    tail = jnp.broadcast_to(tail.reshape(RUNS, 1, RUN, 128), (RUNS, 2, RUN, 128))
    aux = jnp.concatenate([bc, tail], axis=3)
    vmem = pl.BlockSpec(memory_space=pltpu.VMEM)
    anywhere = pl.BlockSpec(memory_space=pl.ANY)
    lanes = [(0, 0), (0, 128 - heads)]
    dma = pltpu.SemaphoreType.DMA
    return pl.pallas_call(
        body,
        out_shape=jax.ShapeDtypeStruct((rows, LOCAL), BF16),
        in_specs=[anywhere] * 3 + [vmem] * 7,
        out_specs=vmem,
        scratch_shapes=[
            pltpu.VMEM((65, RUN, WIDTH), BF16),
            pltpu.VMEM((65, RUN, AUX), BF16),
            pltpu.VMEM((SEG + 8, 128), F32),
            pltpu.VMEM((3, SEG, 128), F32),
            pltpu.VMEM((SEG, WIDTH), BF16),
            pltpu.VMEM((SEG, 256), BF16),
            pltpu.VMEM((SEG, WIDTH), F32),
            pltpu.VMEM((SEG, WIDTH), BF16),
            pltpu.VMEM((SEG, WIDTH), F32),
            pltpu.VMEM((SEG, WIDTH), F32),
            pltpu.VMEM((8, WIDTH), F32),
            pltpu.VMEM((SEGS, 2 * SLICE, 128), BF16),
            pltpu.VMEM((SEGS, 2 * SLICE, 128), BF16),
            pltpu.VMEM((SEGS, SLICE, 128), BF16),
            pltpu.VMEM((SEGS, SLICE, 128), BF16),
            pltpu.VMEM((64, RUN, WIDTH), BF16),
            pltpu.VMEM((RUNS, RUN, LOCAL), BF16),
            pltpu.VMEM((RUNS, RUN, LOCAL), BF16),
            pltpu.VMEM((n_col, 8, 128), F32),
            dma((6,)),
            dma((3,)),
            dma((3,)),
            dma((4,)),
            dma,
            dma,
            dma,
            dma,
            dma,
        ],
        compiler_params=pltpu.CompilerParams(
            collective_id=0, has_side_effects=True, vmem_limit_bytes=40 * 2**20
        ),
    )(
        x_in.reshape(RUNS, RUN, LOCAL),
        aux,
        z_in.reshape(RUNS, RUN, LOCAL),
        conv_x,
        bias_x[None],
        conv_bc.reshape(4, 512),
        bias_bc.reshape(1, 512),
        jnp.pad(rate[None], lanes),
        jnp.pad(dskip[None], lanes),
        norm_gain[None],
    )


def solution(mesh):
    placed = (
        P("seq", "mp"),
        P("seq", None, "mp"),
        P("seq", "mp"),
        P("seq"),
        P(None, "mp"),
        P("mp"),
        P(None, None, "mp"),
        P(None, "mp"),
        P("mp"),
        P("mp"),
        P("seq", "mp"),
        P("mp"),
    )
    return jax.shard_map(
        local, mesh=mesh, in_specs=placed, out_specs=P("seq", "mp"), check_vma=False
    )
```

```python
import jax
import jax.numpy as jnp
from jax import lax
from jax.experimental import pallas as pl
from jax.experimental.pallas import tpu as pltpu
from jax.sharding import PartitionSpec as P

MESH = pl.DeviceIdType.MESH
F32 = jnp.float32
BF16 = jnp.bfloat16

DSTATE = 128
HDIM = 64
SPAN = 256
DI = 8192
EPSILON = 1e-05

RUNS = 16
RUN = 8
HALF = 64
SEGS = 32
SEG = 512
PIECES = 4
WIDTH = 512
LOCAL = 2048
AUX = 384
NB = 1
PART = WIDTH // NB
SLICE = PART // SEGS


def split(value, parts):
    out = []
    for _ in range(parts):
        piece = value.astype(BF16)
        out.append(piece)
        value = value - piece.astype(F32)
    return jnp.concatenate(out, axis=1)


def dot(a, b, dims=((1,), (0,))):
    return lax.dot_general(a, b, (dims, ((), ())), preferred_element_type=F32)


def silu(u):
    return u * lax.logistic(u)


def body(
    x_hbm,
    z_hbm,
    bc_hbm,
    dt_hbm,
    doc_hbm,
    conv_x_hbm,
    bias_x_hbm,
    conv_bc_hbm,
    bias_bc_hbm,
    rate_hbm,
    dskip_hbm,
    gain_hbm,
    out_ref,
    bc_in,
    dt_in,
    doc_in,
    conv_x,
    bias_x,
    conv_bc,
    bias_bc,
    rate,
    dskip,
    gain,
    asend,
    xr,
    ar,
    ext,
    same,
    xc,
    bcc,
    xin,
    xst,
    eout,
    inner,
    srows,
    psend,
    precv,
    sbuf,
    srecv,
    inb,
    inr,
    ysend,
    yrecv,
    zbuf,
    zs,
    part,
    ready_sem,
    send_sem,
    recv_x,
    recv_a,
    share_sem,
    halo_x_sem,
    halo_a_sem,
    pass_sem,
    state_sem,
    back_sem,
    y_sem,
    part_sem,
    z_sem,
    load_sem,
):
    me = lax.axis_index("seq")
    col = lax.axis_index("mp")
    n_col = lax.axis_size("mp")
    half = me // HALF
    t = me % HALF
    q = t // PIECES
    w = t % PIECES
    group = w // 2
    core = t % 2
    chip = t // 2
    seg = q * 2 + half

    def remote(src, dst, sent, got, seq, mp=col):
        return pltpu.make_async_remote_copy(
            src_ref=src,
            dst_ref=dst,
            send_sem=sent,
            recv_sem=got,
            device_id=(seq, mp),
            device_id_type=MESH,
        )

    def signal(sem, seq, mp=col):
        pl.semaphore_signal(sem, inc=1, device_id=(seq, mp), device_id_type=MESH)

    def seg_device(r):
        return (r % 2) * HALF + (r // 2) * PIECES + w

    def take(buf, sem):
        pltpu.make_async_copy(buf, buf, sem).wait()

    loads = [
        pltpu.make_async_copy(src, dst, load_sem.at[k])
        for k, (src, dst) in enumerate(
            [
                (bc_hbm, bc_in),
                (dt_hbm, dt_in),
                (doc_hbm, doc_in),
                (conv_x_hbm, conv_x),
                (bias_x_hbm, bias_x),
                (conv_bc_hbm, conv_bc),
                (bias_bc_hbm, bias_bc),
                (rate_hbm, rate),
                (dskip_hbm, dskip),
                (gain_hbm, gain),
            ]
        )
    ]
    for copy in loads[:3]:
        copy.start()

    barrier = pltpu.get_barrier_semaphore()
    plane, spot = me // 16, me % 16
    for k in range(1, 8):
        signal(barrier, ((plane + k) % 8) * 16 + spot)
    for k in range(1, 16):
        signal(barrier, plane * 16 + (spot + k) % 16)
    for k in range(1, n_col):
        signal(barrier, me, (col + k) % n_col)

    for copy in loads[3:]:
        copy.start()
    z_copy = pltpu.make_async_copy(z_hbm, zbuf, z_sem)
    z_copy.start()
    for copy in loads[:3]:
        copy.wait()

    doc = jnp.broadcast_to(doc_in[...].astype(F32), (128 - 32, 128))
    tail = jnp.transpose(jnp.concatenate([dt_in[...].astype(F32), doc], axis=0))
    tail = tail.reshape(RUNS, RUN, 128).astype(BF16)
    pairs = bc_in[...].astype(F32)
    for k in range(2):
        for n in range(2):
            part_bc = pairs[:, n, k * 128 : k * 128 + 128].astype(BF16)
            asend[:, k, :, n * 128 : n * 128 + 128] = part_bc.reshape(RUNS, RUN, 128)
        asend[:, k, :, 256:] = tail

    pl.semaphore_wait(barrier, 7 + 15 + n_col - 1)
    for k in range(1, 8):
        signal(ready_sem, ((plane + k) % 8) * 16 + spot)
    pl.semaphore_wait(ready_sem, 7)

    kind = t // 63

    def x_block(b, d):
        at = pl.multiple_of((d % PIECES) * WIDTH + b * PART, 128)
        return x_hbm.at[d // PIECES, :, pl.ds(at, PART)]

    def aux_block(d):
        return asend.at[d // PIECES, (d % PIECES) // 2]

    def send_x(b):
        @pl.loop(1, HALF)
        def _(k):
            d = (t + k * 33) % HALF
            remote(
                x_block(b, d), xr.at[b, 1 + t], send_sem.at[0], recv_x.at[b, kind], half * HALF + d
            ).start()

        pltpu.make_async_copy(x_block(b, t), xr.at[b, 1 + t], recv_x.at[b, kind]).start()

    @pl.loop(1, HALF // 2)
    def _(k):
        d = ((chip + k * 17) % 32) * 2 + core
        remote(
            aux_block(d), ar.at[1 + chip, core], send_sem.at[1], recv_a, half * HALF + d
        ).start()

    pltpu.make_async_copy(aux_block(t), ar.at[1 + chip, core], recv_a).start()
    for b in range(NB):
        send_x(b)

    take(ar.at[pl.ds(1, 32), core], recv_a)
    share = remote(
        ar.at[pl.ds(1, 32), core],
        ar.at[pl.ds(1, 32), core],
        share_sem.at[0],
        share_sem.at[1],
        me + 1 - 2 * core,
    )
    share.start()
    share.wait()

    following = seg_device((seg + 1) % SEGS)
    halo_a = remote(ar.at[32, 1], ar.at[0, 1], halo_a_sem.at[0], halo_a_sem.at[1], following)
    halo_a.start()

    def halo_x(b):
        return remote(
            xr.at[b, 64], xr.at[b, 0], halo_x_sem.at[b, 0], halo_x_sem.at[b, 1], following
        )

    for copy in loads[3:]:
        copy.wait()
    none = jnp.zeros((1, 96), F32)
    rates = jnp.concatenate([rate[...], none], axis=1)
    skips = jnp.concatenate([dskip[...], none], axis=1)
    lane = lax.broadcasted_iota(jnp.int32, (128, WIDTH), 1)
    row = lax.broadcasted_iota(jnp.int32, (128, WIDTH), 0)
    spread = (row == w * 8 + lax.shift_right_logical(lane, 6)).astype(F32).astype(BF16)
    spread = jnp.concatenate([spread] * 3, axis=0)

    raw = ar[1:, :, :, 256:384].astype(F32).reshape(SEG, 128)
    step = jnp.maximum(raw, 0.0) + jnp.log1p(jnp.exp(-jnp.abs(raw)))
    log_decay = split(-step * rates, 3)
    tri = (
        lax.broadcasted_iota(jnp.int32, (SPAN, SPAN), 0)
        >= lax.broadcasted_iota(jnp.int32, (SPAN, SPAN), 1)
    ).astype(F32)
    tri_bf = tri.astype(BF16)
    mids, lasts = [], []
    for c in range(2):
        at = slice(c * SPAN, c * SPAN + SPAN)
        sums = dot(tri_bf, log_decay[at])
        decay = sums[:, :128] + sums[:, 128:256] + sums[:, 256:]
        mid, end = decay[127:128], decay[255:256]
        mids.append(mid)
        lasts.append(end)
        into = jnp.exp(mid - decay) * step[at]
        xin[at] = dot(split(into, 2), spread[:256])
        eout[at] = dot(split(jnp.exp(decay - mid), 2), spread[:256])
    rows = jnp.concatenate(
        [
            jnp.exp(mids[0]),
            jnp.exp(mids[1] + lasts[0] - mids[0]),
            jnp.exp(mids[1] + lasts[0]),
            jnp.exp(lasts[0] - mids[0] + lasts[1]),
            jnp.exp(lasts[1] - mids[1]),
            skips,
            jnp.zeros((2, 128), F32),
        ],
        axis=0,
    )
    srows[...] = dot(split(rows, 3), spread)

    take(xr.at[0, pl.ds(64, 1)], recv_x.at[0, 1])
    halo_x(0).start()
    halo_a.wait()

    docs = ar[:, :, :, 256:384].astype(F32).reshape(SEG + 16, 128)[8:]
    docs = jnp.broadcast_to(docs[:, 127:128], (SEG + 8, 128))
    ahead = lax.broadcasted_iota(jnp.int32, (SEG + 8, 128), 0) < 8
    docs = jnp.where(jnp.logical_and(ahead, seg == 0), -1.0, docs)
    ext[...] = docs
    own = ext[8:, :]
    for k in range(1, 4):
        same[k - 1] = (ext[8 - k : 8 - k + SEG, :] == own).astype(F32)
    before = ext[7:8, :]
    last = ext[SEG + 7 : SEG + 8, :]
    from_before = (own == before).astype(F32)
    to_last = (own == last).astype(F32)
    marks = (own == lax.broadcasted_iota(jnp.int32, (SEG, 128), 1).astype(F32)).astype(F32)
    marks = marks.astype(BF16)

    psend[...] = jnp.exp(lasts[0] + lasts[1]) * (before == last).astype(F32)

    @pl.loop(1, SEGS)
    def _(k):
        r = (seg + k * 17) % SEGS
        remote(psend, precv.at[seg], send_sem.at[5], pass_sem, seg_device(r)).start()

    pltpu.make_async_copy(psend, precv.at[seg], pass_sem).start()

    def conv(block, taps, bias):
        ext[...] = block
        total = bias + taps[3:4] * ext[8:, :]
        for k in range(1, 4):
            total = total + taps[3 - k : 4 - k] * ext[8 - k : 8 - k + SEG, :] * same[k - 1]
        return silu(total).astype(BF16)

    for k in range(2):
        at = pl.ds(pl.multiple_of(group * 128, 128), 128)
        block = ar[:, :, :, k * 128 : k * 128 + 128].astype(F32)
        bcc[:, k * 128 : k * 128 + 128] = conv(
            block.reshape(SEG + 16, 128)[8:], conv_bc[:, k, at], bias_bc[k : k + 1, at]
        )
    weighted = (bcc[:, :128].astype(F32) * to_last).astype(BF16)
    reads = (bcc[:, 128:].astype(F32) * from_before).astype(BF16)

    scored = []
    for c, e in ((0, 0), (1, 1), (1, 0)):
        at, to = slice(c * SPAN, c * SPAN + SPAN), slice(e * SPAN, e * SPAN + SPAN)
        seen = dot(marks[at], marks[to], ((1,), (1,)))
        if c == e:
            seen = seen * tri
        scored.append((dot(bcc[at, 128:], bcc[to, :128], ((1,), (1,))) * seen).astype(BF16))

    for b in range(NB):
        here = slice(b * PART, b * PART + PART)
        if b:
            take(xr.at[b, pl.ds(64, 1)], recv_x.at[b, 1])
            halo_x(b).start()
        take(xr.at[b, pl.ds(1, 63)], recv_x.at[b, 0])
        halo_x(b).wait()
        for j in range(PART // 128):
            at = slice(b * PART + j * 128, b * PART + j * 128 + 128)
            far = pl.ds(pl.multiple_of(w * WIDTH + b * PART + j * 128, 128), 128)
            mixed = conv(
                xr[b, :, :, j * 128 : j * 128 + 128].astype(F32).reshape(SEG + 8, 128),
                conv_x[:, far],
                bias_x[:, far],
            )
            xc[:, at] = mixed
            scaled = mixed.astype(F32) * xin[:, at]
            xst[:SPAN, at] = (scaled[:SPAN] * srows[3:4, at]).astype(BF16)
            xst[SPAN:, at] = (scaled[SPAN:] * srows[4:5, at]).astype(BF16)
            xin[:, at] = scaled
        state = dot(xst[:, here], weighted, ((0,), (0,)))
        sbuf[b] = state.reshape(SEGS, SLICE, 128).astype(BF16)

        @pl.loop(1, SEGS)
        def _(k):
            r = (seg + k * 17) % SEGS
            remote(
                sbuf.at[b, r], srecv.at[b, seg], send_sem.at[2], state_sem.at[b], seg_device(r)
            ).start()

        pltpu.make_async_copy(sbuf.at[b, seg], srecv.at[b, seg], state_sem.at[b]).start()

        inner[:SPAN, here] = dot(scored[0], xin[:SPAN, here].astype(BF16))
        inner[SPAN:, here] = (
            dot(scored[1], xin[SPAN:, here].astype(BF16))
            + dot(scored[2], xin[:SPAN, here].astype(BF16)) * srows[1:2, here]
        )

    z_copy.wait()
    for k in range(RUNS):
        zs[k * RUN : k * RUN + RUN] = silu(zbuf[k].astype(F32))

    take(precv, pass_sem)
    factors = precv[...].reshape(SEGS, 128)
    lanes = lax.broadcasted_iota(jnp.int32, (SEGS, 128), 1)
    for b in range(NB):
        head = lanes == w * 8 + b * (8 // NB) + seg * SLICE // HDIM
        factor = jnp.sum(jnp.where(head, factors, 0.0), axis=1, keepdims=True)
        take(srecv.at[b], state_sem.at[b])
        carried = jnp.zeros((SLICE, 128), F32)
        for g in range(SEGS):
            inb[b, g] = carried.astype(BF16)
            carried = srecv[b, g].astype(F32) + factor[g : g + 1] * carried

        @pl.loop(1, SEGS)
        def _(k):
            r = (seg + k * 17) % SEGS
            remote(
                inb.at[b, r], inr.at[b, seg], send_sem.at[3], back_sem.at[b], seg_device(r)
            ).start()

        pltpu.make_async_copy(inb.at[b, seg], inr.at[b, seg], back_sem.at[b]).start()

    for b in range(NB):
        here = slice(b * PART, b * PART + PART)
        take(inr.at[b], back_sem.at[b])
        incoming = inr[b].astype(F32).reshape(PART, 128).astype(BF16)
        for c in range(2):
            at = slice(c * SPAN, c * SPAN + SPAN)
            cross = dot(reads[at], incoming, ((1,), (1,))) * srows[2 * c : 2 * c + 1, here]
            y = (inner[at, here] + cross) * eout[at, here]
            y = y + srows[5:6, here] * xc[at, here].astype(F32)
            ysend[b, c * 32 : c * 32 + 32] = y.reshape(32, RUN, PART).astype(BF16)
        place = yrecv.at[b, q, :, pl.ds(pl.multiple_of(w * PART, 128), PART)]

        @pl.loop(1, HALF)
        def _(k):
            d = (t + k * 33) % HALF
            remote(ysend.at[b, d], place, send_sem.at[4], y_sem.at[b], half * HALF + d).start()

        pltpu.make_async_copy(ysend.at[b, t], place, y_sem.at[b]).start()

    sums = jnp.zeros((RUNS * RUN, PART), F32)
    for b in range(NB):
        take(yrecv.at[b], y_sem.at[b])
        for k in range(PIECES):
            at = slice(k * WIDTH + b * PART, k * WIDTH + b * PART + PART)
            y = yrecv[b, :, :, k * PART : k * PART + PART].astype(F32)
            gated = y.reshape(RUNS * RUN, PART) * zs[:, at]
            zs[:, at] = gated
            sums = sums + gated * gated
    square = jnp.sum(sums, axis=1, keepdims=True)
    part[col] = jnp.transpose(jnp.broadcast_to(square, (128, 128)))[:8]
    for k in range(1, n_col):
        remote(
            part.at[col], part.at[col], send_sem.at[6], part_sem, me, (col + k) % n_col
        ).start()
    take(part.at[pl.ds(0, n_col - 1)], part_sem)
    total = jnp.sum(part[...], axis=0)
    total = jnp.transpose(jnp.broadcast_to(total[:1], (128, 128)))[:, :1]
    scale = lax.rsqrt(total / DI + EPSILON)
    for k in range(LOCAL // 512):
        at = slice(k * 512, k * 512 + 512)
        out_ref[:, at] = (zs[:, at] * scale * gain[:, at]).astype(BF16)

    for b in range(NB):
        take(xr.at[b, pl.ds(0, 63)], send_sem.at[0])
        take(sbuf.at[b, pl.ds(0, 31)], send_sem.at[2])
        take(inb.at[b, pl.ds(0, 31)], send_sem.at[3])
        take(ysend.at[b, pl.ds(0, 63)], send_sem.at[4])
    take(ar.at[pl.ds(0, 31), 0], send_sem.at[1])
    take(precv.at[pl.ds(0, 31)], send_sem.at[5])
    take(part.at[pl.ds(0, n_col - 1)], send_sem.at[6])


def local(
    x_in, bc_in, dt_raw, doc_id, conv_x, bias_x, conv_bc, bias_bc, rate, dskip, z_in, norm_gain
):
    n_col = lax.axis_size("mp")
    rows = x_in.shape[0]
    heads = rate.shape[0]
    vmem = pl.BlockSpec(memory_space=pltpu.VMEM)
    hbm = pl.BlockSpec(memory_space=pltpu.HBM)
    dma = pltpu.SemaphoreType.DMA
    return pl.pallas_call(
        body,
        out_shape=jax.ShapeDtypeStruct((rows, LOCAL), BF16),
        in_specs=[hbm] * 12,
        out_specs=vmem,
        scratch_shapes=[
            pltpu.VMEM((rows, 2, 256), BF16),
            pltpu.VMEM((heads, rows), BF16),
            pltpu.VMEM((1, rows), jnp.int32),
            pltpu.VMEM((4, LOCAL), F32),
            pltpu.VMEM((1, LOCAL), F32),
            pltpu.VMEM((4, 2, 256), F32),
            pltpu.VMEM((2, 256), F32),
            pltpu.VMEM((1, heads), F32),
            pltpu.VMEM((1, heads), F32),
            pltpu.VMEM((1, LOCAL), F32),
            pltpu.VMEM((RUNS, 2, RUN, AUX), BF16),
            pltpu.VMEM((NB, 65, RUN, PART), BF16),
            pltpu.VMEM((33, 2, RUN, AUX), BF16),
            pltpu.VMEM((SEG + 8, 128), F32),
            pltpu.VMEM((3, SEG, 128), F32),
            pltpu.VMEM((SEG, WIDTH), BF16),
            pltpu.VMEM((SEG, 256), BF16),
            pltpu.VMEM((SEG, WIDTH), F32),
            pltpu.VMEM((SEG, WIDTH), BF16),
            pltpu.VMEM((SEG, WIDTH), F32),
            pltpu.VMEM((SEG, WIDTH), F32),
            pltpu.VMEM((8, WIDTH), F32),
            pltpu.VMEM((1, 128), F32),
            pltpu.VMEM((SEGS, 1, 128), F32),
            pltpu.VMEM((NB, SEGS, SLICE, 128), BF16),
            pltpu.VMEM((NB, SEGS, SLICE, 128), BF16),
            pltpu.VMEM((NB, SEGS, SLICE, 128), BF16),
            pltpu.VMEM((NB, SEGS, SLICE, 128), BF16),
            pltpu.VMEM((NB, 64, RUN, PART), BF16),
            pltpu.VMEM((NB, RUNS, RUN, PIECES * PART), BF16),
            pltpu.VMEM((RUNS, RUN, LOCAL), BF16),
            pltpu.VMEM((RUNS * RUN, LOCAL), F32),
            pltpu.VMEM((n_col, 8, 128), F32),
            pltpu.SemaphoreType.REGULAR,
            dma((7,)),
            dma((NB, 2)),
            dma,
            dma((2,)),
            dma((NB, 2)),
            dma((2,)),
            dma,
            dma((NB,)),
            dma((NB,)),
            dma((NB,)),
            dma,
            dma,
            dma((10,)),
        ],
        compiler_params=pltpu.CompilerParams(
            collective_id=0, has_side_effects=True, vmem_limit_bytes=60 * 2**20
        ),
    )(
        x_in.reshape(RUNS, RUN, LOCAL),
        z_in.reshape(RUNS, RUN, LOCAL),
        bc_in,
        dt_raw.T,
        doc_id[None],
        conv_x,
        bias_x[None],
        conv_bc,
        bias_bc,
        rate[None],
        dskip[None],
        norm_gain[None],
    )


def solution(mesh):
    placed = (
        P("seq", "mp"),
        P("seq", None, "mp"),
        P("seq", "mp"),
        P("seq"),
        P(None, "mp"),
        P("mp"),
        P(None, None, "mp"),
        P(None, "mp"),
        P("mp"),
        P("mp"),
        P("seq", "mp"),
        P("mp"),
    )
    return jax.shard_map(
        local, mesh=mesh, in_specs=placed, out_specs=P("seq", "mp"), check_vma=False
    )
```

```python
import jax
import jax.numpy as jnp
from jax import lax
from jax.experimental import pallas as pl
from jax.experimental.pallas import tpu as pltpu
from jax.sharding import PartitionSpec as P

MESH = pl.DeviceIdType.MESH
F32 = jnp.float32
BF16 = jnp.bfloat16

DSTATE = 128
HDIM = 64
SPAN = 256
DI = 8192
EPSILON = 1e-05

RUNS = 16
RUN = 8
HALF = 64
SEGS = 32
SEG = 512
PIECES = 4
WIDTH = 512
LOCAL = 2048
AUX = 384
NB = 2
PART = WIDTH // NB
SLICE = PART // SEGS
CUTS = (24, 64)


def split(value, parts):
    out = []
    for _ in range(parts):
        piece = value.astype(BF16)
        out.append(piece)
        value = value - piece.astype(F32)
    return jnp.concatenate(out, axis=1)


def dot(a, b, dims=((1,), (0,))):
    return lax.dot_general(a, b, (dims, ((), ())), preferred_element_type=F32)


def silu(u):
    return u * lax.logistic(u)


def body(
    x_hbm,
    z_hbm,
    bc_hbm,
    dt_hbm,
    doc_hbm,
    conv_x_hbm,
    bias_x_hbm,
    conv_bc_hbm,
    bias_bc_hbm,
    rate_hbm,
    dskip_hbm,
    gain_hbm,
    out_ref,
    bc_in,
    dt_in,
    doc_in,
    conv_x,
    bias_x,
    conv_bc,
    bias_bc,
    rate,
    dskip,
    gain,
    asend,
    xr,
    ar,
    ext,
    same,
    xc,
    bcc,
    xin,
    xst,
    eout,
    inner,
    srows,
    psend,
    precv,
    sbuf,
    srecv,
    inb,
    inr,
    ysend,
    yrecv,
    zbuf,
    zs,
    part,
    ready_sem,
    send_sem,
    recv_x,
    recv_a,
    share_sem,
    halo_x_sem,
    halo_a_sem,
    pass_sem,
    state_sem,
    back_sem,
    y_sem,
    part_sem,
    z_sem,
    load_sem,
):
    me = lax.axis_index("seq")
    col = lax.axis_index("mp")
    n_col = lax.axis_size("mp")
    half = me // HALF
    t = me % HALF
    q = t // PIECES
    w = t % PIECES
    group = w // 2
    core = t % 2
    chip = t // 2
    seg = q * 2 + half

    def remote(src, dst, sent, got, seq, mp=col):
        return pltpu.make_async_remote_copy(
            src_ref=src,
            dst_ref=dst,
            send_sem=sent,
            recv_sem=got,
            device_id=(seq, mp),
            device_id_type=MESH,
        )

    def signal(sem, seq, mp=col):
        pl.semaphore_signal(sem, inc=1, device_id=(seq, mp), device_id_type=MESH)

    def seg_device(r):
        return (r % 2) * HALF + (r // 2) * PIECES + w

    def take(buf, sem):
        pltpu.make_async_copy(buf, buf, sem).wait()

    loads = [
        pltpu.make_async_copy(src, dst, load_sem.at[k])
        for k, (src, dst) in enumerate(
            [
                (bc_hbm, bc_in),
                (dt_hbm, dt_in),
                (doc_hbm, doc_in),
                (conv_x_hbm, conv_x),
                (bias_x_hbm, bias_x),
                (conv_bc_hbm, conv_bc),
                (bias_bc_hbm, bias_bc),
                (rate_hbm, rate),
                (dskip_hbm, dskip),
                (gain_hbm, gain),
            ]
        )
    ]
    for copy in loads[:3]:
        copy.start()

    barrier = pltpu.get_barrier_semaphore()
    plane, spot = me // 16, me % 16
    for k in range(1, 8):
        signal(barrier, ((plane + k) % 8) * 16 + spot)
    for k in range(1, 16):
        signal(barrier, plane * 16 + (spot + k) % 16)
    for k in range(1, n_col):
        signal(barrier, me, (col + k) % n_col)

    for copy in loads[3:]:
        copy.start()
    z_copy = pltpu.make_async_copy(z_hbm, zbuf, z_sem)
    z_copy.start()
    pl.semaphore_wait(barrier, 7 + 15 + n_col - 1)
    for k in range(1, 8):
        signal(ready_sem, ((plane + k) % 8) * 16 + spot)

    for copy in loads[:3]:
        copy.wait()

    doc = jnp.broadcast_to(doc_in[...].astype(F32), (128 - 32, 128))
    tail = jnp.transpose(jnp.concatenate([dt_in[...].astype(F32), doc], axis=0))
    tail = tail.reshape(RUNS, RUN, 128).astype(BF16)
    pairs = bc_in[...].astype(F32)
    for k in range(2):
        for n in range(2):
            part_bc = pairs[:, n, k * 128 : k * 128 + 128].astype(BF16)
            asend[:, k, :, n * 128 : n * 128 + 128] = part_bc.reshape(RUNS, RUN, 128)
        asend[:, k, :, 256:] = tail

    pl.semaphore_wait(ready_sem, 7)

    kind = t // 63

    def x_block(b, d):
        at = pl.multiple_of((d % PIECES) * WIDTH + b * PART, 128)
        return x_hbm.at[d // PIECES, :, pl.ds(at, PART)]

    def aux_block(d):
        return asend.at[d // PIECES, (d % PIECES) // 2]

    def send_x(b, first, stop):
        @pl.loop(first, stop)
        def _(k):
            d = (t + k * 37) % HALF
            remote(
                x_block(b, d), xr.at[b, 1 + t], send_sem.at[0], recv_x.at[b, kind], half * HALF + d
            ).start()

        if first == 1:
            pltpu.make_async_copy(x_block(b, t), xr.at[b, 1 + t], recv_x.at[b, kind]).start()

    @pl.loop(1, HALF // 2)
    def _(k):
        d = ((chip + k * 17) % 32) * 2 + core
        remote(
            aux_block(d), ar.at[1 + chip, core], send_sem.at[1], recv_a, half * HALF + d
        ).start()

    pltpu.make_async_copy(aux_block(t), ar.at[1 + chip, core], recv_a).start()
    send_x(0, 1, CUTS[0])

    z_copy.wait()
    for k in range(RUNS):
        zs[k * RUN : k * RUN + RUN] = silu(zbuf[k].astype(F32))
    send_x(0, CUTS[0], CUTS[1])

    take(ar.at[pl.ds(1, 32), core], recv_a)
    share = remote(
        ar.at[pl.ds(1, 32), core],
        ar.at[pl.ds(1, 32), core],
        share_sem.at[0],
        share_sem.at[1],
        me + 1 - 2 * core,
    )
    share.start()
    if CUTS[1] < HALF:
        send_x(0, CUTS[1], HALF)
    for b in range(1, NB):
        send_x(b, 1, HALF // 2)
    share.wait()

    following = seg_device((seg + 1) % SEGS)
    halo_a = remote(ar.at[32, 1], ar.at[0, 1], halo_a_sem.at[0], halo_a_sem.at[1], following)
    halo_a.start()

    def halo_x(b):
        return remote(
            xr.at[b, 64], xr.at[b, 0], halo_x_sem.at[b, 0], halo_x_sem.at[b, 1], following
        )

    for copy in loads[3:]:
        copy.wait()
    none = jnp.zeros((1, 96), F32)
    rates = jnp.concatenate([rate[...], none], axis=1)
    skips = jnp.concatenate([dskip[...], none], axis=1)
    lane = lax.broadcasted_iota(jnp.int32, (128, WIDTH), 1)
    row = lax.broadcasted_iota(jnp.int32, (128, WIDTH), 0)
    spread = (row == w * 8 + lax.shift_right_logical(lane, 6)).astype(F32).astype(BF16)
    spread = jnp.concatenate([spread] * 3, axis=0)

    raw = ar[1:, :, :, 256:384].astype(F32).reshape(SEG, 128)
    step = jnp.maximum(raw, 0.0) + jnp.log1p(jnp.exp(-jnp.abs(raw)))
    log_decay = split(-step * rates, 3)
    tri = (
        lax.broadcasted_iota(jnp.int32, (SPAN, SPAN), 0)
        >= lax.broadcasted_iota(jnp.int32, (SPAN, SPAN), 1)
    ).astype(F32)
    tri_bf = tri.astype(BF16)
    mids, lasts = [], []
    for c in range(2):
        at = slice(c * SPAN, c * SPAN + SPAN)
        sums = dot(tri_bf, log_decay[at])
        decay = sums[:, :128] + sums[:, 128:256] + sums[:, 256:]
        mid, end = decay[127:128], decay[255:256]
        mids.append(mid)
        lasts.append(end)
        into = jnp.exp(mid - decay) * step[at]
        xin[at] = dot(split(into, 2), spread[:256])
        eout[at] = dot(split(jnp.exp(decay - mid), 2), spread[:256])
    rows = jnp.concatenate(
        [
            jnp.exp(mids[0]),
            jnp.exp(mids[1] + lasts[0] - mids[0]),
            jnp.exp(mids[1] + lasts[0]),
            jnp.exp(lasts[0] - mids[0] + lasts[1]),
            jnp.exp(lasts[1] - mids[1]),
            skips,
            jnp.zeros((2, 128), F32),
        ],
        axis=0,
    )
    srows[...] = dot(split(rows, 3), spread)

    take(xr.at[0, pl.ds(64, 1)], recv_x.at[0, 1])
    halo_x(0).start()
    for b in range(1, NB):
        send_x(b, HALF // 2, HALF)
    halo_a.wait()

    docs = ar[:, :, :, 256:384].astype(F32).reshape(SEG + 16, 128)[8:]
    docs = jnp.broadcast_to(docs[:, 127:128], (SEG + 8, 128))
    ahead = lax.broadcasted_iota(jnp.int32, (SEG + 8, 128), 0) < 8
    docs = jnp.where(jnp.logical_and(ahead, seg == 0), -1.0, docs)
    ext[...] = docs
    own = ext[8:, :]
    for k in range(1, 4):
        same[k - 1] = (ext[8 - k : 8 - k + SEG, :] == own).astype(F32)
    before = ext[7:8, :]
    last = ext[SEG + 7 : SEG + 8, :]
    from_before = (own == before).astype(F32)
    to_last = (own == last).astype(F32)
    marks = (own == lax.broadcasted_iota(jnp.int32, (SEG, 128), 1).astype(F32)).astype(F32)
    marks = marks.astype(BF16)

    psend[...] = jnp.exp(lasts[0] + lasts[1]) * (before == last).astype(F32)

    @pl.loop(1, SEGS)
    def _(k):
        r = (seg + k * 17) % SEGS
        remote(psend, precv.at[seg], send_sem.at[5], pass_sem, seg_device(r)).start()

    pltpu.make_async_copy(psend, precv.at[seg], pass_sem).start()

    def conv(block, taps, bias):
        size = block.shape[0] - 8
        ext[: size + 8] = block
        total = bias + taps[3:4] * block[8:]
        for k in range(1, 4):
            moved = ext[8 - k : 8 - k + size, :] * same[k - 1, :size]
            total = total + taps[3 - k : 4 - k] * moved
        return silu(total).astype(BF16)

    for k in range(2):
        at = pl.ds(pl.multiple_of(group * 128, 128), 128)
        block = ar[:, :, :, k * 128 : k * 128 + 128].astype(F32)
        bcc[:, k * 128 : k * 128 + 128] = conv(
            block.reshape(SEG + 16, 128)[8:], conv_bc[:, k, at], bias_bc[k : k + 1, at]
        )
    weighted = (bcc[:, :128].astype(F32) * to_last).astype(BF16)
    reads = (bcc[:, 128:].astype(F32) * from_before).astype(BF16)

    scored = []
    for c, e in ((0, 0), (1, 1), (1, 0)):
        at, to = slice(c * SPAN, c * SPAN + SPAN), slice(e * SPAN, e * SPAN + SPAN)
        seen = dot(marks[at], marks[to], ((1,), (1,)))
        if c == e:
            seen = seen * tri
        scored.append((dot(bcc[at, 128:], bcc[to, :128], ((1,), (1,))) * seen).astype(BF16))

    for b in range(NB):
        here = slice(b * PART, b * PART + PART)
        take(xr.at[b, pl.ds(1, 63)], recv_x.at[b, 0])
        into = xin[:16, here]
        for j in range(PART // 128):
            at = slice(b * PART + j * 128, b * PART + j * 128 + 128)
            far = pl.ds(pl.multiple_of(w * WIDTH + b * PART + j * 128, 128), 128)
            block = xr[b, 1:, :, j * 128 : j * 128 + 128].astype(F32).reshape(SEG, 128)
            block = jnp.concatenate([jnp.zeros((8, 128), F32), block], axis=0)
            mixed = conv(block, conv_x[:, far], bias_x[:, far])
            xc[:, at] = mixed
            scaled = mixed.astype(F32) * xin[:, at]
            xst[:SPAN, at] = (scaled[:SPAN] * srows[3:4, at]).astype(BF16)
            xst[SPAN:, at] = (scaled[SPAN:] * srows[4:5, at]).astype(BF16)
            xin[:, at] = scaled
        if b + 1 < NB:
            take(xr.at[b + 1, pl.ds(64, 1)], recv_x.at[b + 1, 1])
            halo_x(b + 1).start()
        halo_x(b).wait()
        for j in range(PART // 128):
            at = slice(b * PART + j * 128, b * PART + j * 128 + 128)
            far = pl.ds(pl.multiple_of(w * WIDTH + b * PART + j * 128, 128), 128)
            block = xr[b, :3, :, j * 128 : j * 128 + 128].astype(F32).reshape(24, 128)
            mixed = conv(block, conv_x[:, far], bias_x[:, far])
            xc[:16, at] = mixed
            scaled = mixed.astype(F32) * into[:, j * 128 : j * 128 + 128]
            xst[:16, at] = (scaled * srows[3:4, at]).astype(BF16)
            xin[:16, at] = scaled
        state = dot(xst[:, here], weighted, ((0,), (0,)))
        sbuf[b] = state.reshape(SEGS, SLICE, 128).astype(BF16)

        @pl.loop(1, SEGS)
        def _(k):
            r = (seg + k * 17) % SEGS
            remote(
                sbuf.at[b, r], srecv.at[b, seg], send_sem.at[2], state_sem.at[b], seg_device(r)
            ).start()

        pltpu.make_async_copy(sbuf.at[b, seg], srecv.at[b, seg], state_sem.at[b]).start()

        inner[:SPAN, here] = dot(scored[0], xin[:SPAN, here].astype(BF16))
        inner[SPAN:, here] = (
            dot(scored[1], xin[SPAN:, here].astype(BF16))
            + dot(scored[2], xin[:SPAN, here].astype(BF16)) * srows[1:2, here]
        )

    take(precv, pass_sem)
    factors = precv[...].reshape(SEGS, 128)
    lanes = lax.broadcasted_iota(jnp.int32, (SEGS, 128), 1)
    for b in range(NB):
        head = lanes == w * 8 + b * (8 // NB) + seg * SLICE // HDIM
        factor = jnp.sum(jnp.where(head, factors, 0.0), axis=1, keepdims=True)
        take(srecv.at[b], state_sem.at[b])
        carried = jnp.zeros((SLICE, 128), F32)
        for g in range(SEGS):
            inb[b, g] = carried.astype(BF16)
            carried = srecv[b, g].astype(F32) + factor[g : g + 1] * carried

        @pl.loop(1, SEGS)
        def _(k):
            r = (seg + k * 17) % SEGS
            remote(
                inb.at[b, r], inr.at[b, seg], send_sem.at[3], back_sem.at[b], seg_device(r)
            ).start()

        pltpu.make_async_copy(inb.at[b, seg], inr.at[b, seg], back_sem.at[b]).start()

    for b in range(NB):
        here = slice(b * PART, b * PART + PART)
        take(inr.at[b], back_sem.at[b])
        incoming = inr[b].astype(F32).reshape(PART, 128).astype(BF16)
        for c in range(2):
            at = slice(c * SPAN, c * SPAN + SPAN)
            cross = dot(reads[at], incoming, ((1,), (1,))) * srows[2 * c : 2 * c + 1, here]
            y = (inner[at, here] + cross) * eout[at, here]
            y = y + srows[5:6, here] * xc[at, here].astype(F32)
            ysend[b, c * 32 : c * 32 + 32] = y.reshape(32, RUN, PART).astype(BF16)
        place = yrecv.at[b, q, :, pl.ds(pl.multiple_of(w * PART, 128), PART)]

        @pl.loop(1, HALF)
        def _(k):
            d = (t + k * 37) % HALF
            remote(ysend.at[b, d], place, send_sem.at[4], y_sem.at[b], half * HALF + d).start()

        pltpu.make_async_copy(ysend.at[b, t], place, y_sem.at[b]).start()

    sums = jnp.zeros((RUNS * RUN, PART), F32)
    for b in range(NB):
        take(yrecv.at[b], y_sem.at[b])
        for k in range(PIECES):
            at = slice(k * WIDTH + b * PART, k * WIDTH + b * PART + PART)
            y = yrecv[b, :, :, k * PART : k * PART + PART].astype(F32)
            gated = y.reshape(RUNS * RUN, PART) * zs[:, at]
            zs[:, at] = gated
            sums = sums + gated * gated
    square = jnp.sum(sums, axis=1, keepdims=True)
    part[col] = jnp.transpose(jnp.broadcast_to(square, (128, 128)))[:8]
    for k in range(1, n_col):
        remote(
            part.at[col], part.at[col], send_sem.at[6], part_sem, me, (col + k) % n_col
        ).start()
    take(part.at[pl.ds(0, n_col - 1)], part_sem)
    total = jnp.sum(part[...], axis=0)
    total = jnp.transpose(jnp.broadcast_to(total[:1], (128, 128)))[:, :1]
    scale = lax.rsqrt(total / DI + EPSILON)
    for k in range(LOCAL // 512):
        at = slice(k * 512, k * 512 + 512)
        out_ref[:, at] = (zs[:, at] * scale * gain[:, at]).astype(BF16)

    for b in range(NB):
        take(xr.at[b, pl.ds(0, 63)], send_sem.at[0])
        take(sbuf.at[b, pl.ds(0, 31)], send_sem.at[2])
        take(inb.at[b, pl.ds(0, 31)], send_sem.at[3])
        take(ysend.at[b, pl.ds(0, 63)], send_sem.at[4])
    take(ar.at[pl.ds(0, 31), 0], send_sem.at[1])
    take(precv.at[pl.ds(0, 31)], send_sem.at[5])
    take(part.at[pl.ds(0, n_col - 1)], send_sem.at[6])


def local(
    x_in, bc_in, dt_raw, doc_id, conv_x, bias_x, conv_bc, bias_bc, rate, dskip, z_in, norm_gain
):
    n_col = lax.axis_size("mp")
    rows = x_in.shape[0]
    heads = rate.shape[0]
    vmem = pl.BlockSpec(memory_space=pltpu.VMEM)
    hbm = pl.BlockSpec(memory_space=pltpu.HBM)
    dma = pltpu.SemaphoreType.DMA
    return pl.pallas_call(
        body,
        out_shape=jax.ShapeDtypeStruct((rows, LOCAL), BF16),
        in_specs=[hbm] * 12,
        out_specs=vmem,
        scratch_shapes=[
            pltpu.VMEM((rows, 2, 256), BF16),
            pltpu.VMEM((heads, rows), BF16),
            pltpu.VMEM((1, rows), jnp.int32),
            pltpu.VMEM((4, LOCAL), F32),
            pltpu.VMEM((1, LOCAL), F32),
            pltpu.VMEM((4, 2, 256), F32),
            pltpu.VMEM((2, 256), F32),
            pltpu.VMEM((1, heads), F32),
            pltpu.VMEM((1, heads), F32),
            pltpu.VMEM((1, LOCAL), F32),
            pltpu.VMEM((RUNS, 2, RUN, AUX), BF16),
            pltpu.VMEM((NB, 65, RUN, PART), BF16),
            pltpu.VMEM((33, 2, RUN, AUX), BF16),
            pltpu.VMEM((SEG + 8, 128), F32),
            pltpu.VMEM((3, SEG, 128), F32),
            pltpu.VMEM((SEG, WIDTH), BF16),
            pltpu.VMEM((SEG, 256), BF16),
            pltpu.VMEM((SEG, WIDTH), F32),
            pltpu.VMEM((SEG, WIDTH), BF16),
            pltpu.VMEM((SEG, WIDTH), F32),
            pltpu.VMEM((SEG, WIDTH), F32),
            pltpu.VMEM((8, WIDTH), F32),
            pltpu.VMEM((1, 128), F32),
            pltpu.VMEM((SEGS, 1, 128), F32),
            pltpu.VMEM((NB, SEGS, SLICE, 128), BF16),
            pltpu.VMEM((NB, SEGS, SLICE, 128), BF16),
            pltpu.VMEM((NB, SEGS, SLICE, 128), BF16),
            pltpu.VMEM((NB, SEGS, SLICE, 128), BF16),
            pltpu.VMEM((NB, 64, RUN, PART), BF16),
            pltpu.VMEM((NB, RUNS, RUN, PIECES * PART), BF16),
            pltpu.VMEM((RUNS, RUN, LOCAL), BF16),
            pltpu.VMEM((RUNS * RUN, LOCAL), F32),
            pltpu.VMEM((n_col, 8, 128), F32),
            pltpu.SemaphoreType.REGULAR,
            dma((7,)),
            dma((NB, 2)),
            dma,
            dma((2,)),
            dma((NB, 2)),
            dma((2,)),
            dma,
            dma((NB,)),
            dma((NB,)),
            dma((NB,)),
            dma,
            dma,
            dma((10,)),
        ],
        compiler_params=pltpu.CompilerParams(
            collective_id=0, has_side_effects=True, vmem_limit_bytes=60 * 2**20
        ),
    )(
        x_in.reshape(RUNS, RUN, LOCAL),
        z_in.reshape(RUNS, RUN, LOCAL),
        bc_in,
        dt_raw.T,
        doc_id[None],
        conv_x,
        bias_x[None],
        conv_bc,
        bias_bc,
        rate[None],
        dskip[None],
        norm_gain[None],
    )


def solution(mesh):
    placed = (
        P("seq", "mp"),
        P("seq", None, "mp"),
        P("seq", "mp"),
        P("seq"),
        P(None, "mp"),
        P("mp"),
        P(None, None, "mp"),
        P(None, "mp"),
        P("mp"),
        P("mp"),
        P("seq", "mp"),
        P("mp"),
    )
    return jax.shard_map(
        local, mesh=mesh, in_specs=placed, out_specs=P("seq", "mp"), check_vma=False
    )
```

```python
import jax
import jax.numpy as jnp
from jax import lax
from jax.experimental import pallas as pl
from jax.experimental.pallas import tpu as pltpu
from jax.sharding import PartitionSpec as P

MESH = pl.DeviceIdType.MESH
F32 = jnp.float32
BF16 = jnp.bfloat16

DSTATE = 128
HDIM = 64
SPAN = 256
DI = 8192
EPSILON = 1e-05

RUNS = 16
RUN = 8
HALF = 64
SEGS = 32
SEG = 512
PIECES = 4
WIDTH = 512
LOCAL = 2048
AUX = 384
NB = 2
PART = WIDTH // NB
SLICE = PART // SEGS
CUTS = (24, 64)


def split(value, parts):
    out = []
    for _ in range(parts):
        piece = value.astype(BF16)
        out.append(piece)
        value = value - piece.astype(F32)
    return jnp.concatenate(out, axis=1)


def dot(a, b, dims=((1,), (0,))):
    return lax.dot_general(a, b, (dims, ((), ())), preferred_element_type=F32)


def silu(u):
    return u * lax.logistic(u)


def body(
    x_hbm,
    z_hbm,
    bc_hbm,
    dt_hbm,
    doc_hbm,
    conv_x_hbm,
    bias_x_hbm,
    conv_bc_hbm,
    bias_bc_hbm,
    rate_hbm,
    dskip_hbm,
    gain_hbm,
    out_ref,
    bc_in,
    dt_in,
    doc_in,
    conv_x,
    bias_x,
    conv_bc,
    bias_bc,
    rate,
    dskip,
    gain,
    asend,
    xr,
    ar,
    ext,
    same,
    xc,
    bcc,
    xin,
    xst,
    eout,
    inner,
    srows,
    psend,
    precv,
    sbuf,
    srecv,
    inb,
    inr,
    ysend,
    yrecv,
    zbuf,
    zs,
    part,
    ready_sem,
    send_sem,
    recv_x,
    recv_a,
    share_sem,
    halo_x_sem,
    halo_a_sem,
    pass_sem,
    state_sem,
    back_sem,
    y_sem,
    part_sem,
    z_sem,
    load_sem,
):
    me = lax.axis_index("seq")
    col = lax.axis_index("mp")
    n_col = lax.axis_size("mp")
    half = me // HALF
    t = me % HALF
    flip = 48 * half
    role = t ^ flip
    q = role // PIECES
    w = role % PIECES
    group = w // 2
    core = t % 2
    chip = t // 2
    seg = q * 2 + half

    def remote(src, dst, sent, got, seq, mp=col):
        return pltpu.make_async_remote_copy(
            src_ref=src,
            dst_ref=dst,
            send_sem=sent,
            recv_sem=got,
            device_id=(seq, mp),
            device_id_type=MESH,
        )

    def signal(sem, seq, mp=col):
        pl.semaphore_signal(sem, inc=1, device_id=(seq, mp), device_id_type=MESH)

    def seg_device(r):
        return (r % 2) * HALF + (((r // 2) * PIECES + w) ^ (48 * (r % 2)))

    def take(buf, sem):
        pltpu.make_async_copy(buf, buf, sem).wait()

    loads = [
        pltpu.make_async_copy(src, dst, load_sem.at[k])
        for k, (src, dst) in enumerate(
            [
                (bc_hbm, bc_in),
                (dt_hbm, dt_in),
                (doc_hbm, doc_in),
                (conv_x_hbm, conv_x),
                (bias_x_hbm, bias_x),
                (conv_bc_hbm, conv_bc),
                (bias_bc_hbm, bias_bc),
                (rate_hbm, rate),
                (dskip_hbm, dskip),
                (gain_hbm, gain),
            ]
        )
    ]
    for copy in loads[:3]:
        copy.start()

    barrier = pltpu.get_barrier_semaphore()
    plane, spot = me // 16, me % 16
    for k in range(1, 8):
        signal(barrier, ((plane + k) % 8) * 16 + spot)
    for k in range(1, 16):
        signal(barrier, plane * 16 + (spot + k) % 16)
    for k in range(1, n_col):
        signal(barrier, me, (col + k) % n_col)

    for copy in loads[3:]:
        copy.start()
    z_copy = pltpu.make_async_copy(z_hbm, zbuf, z_sem)
    z_copy.start()
    pl.semaphore_wait(barrier, 7 + 15 + n_col - 1)
    for k in range(1, 8):
        signal(ready_sem, ((plane + k) % 8) * 16 + spot)

    for copy in loads[:3]:
        copy.wait()

    doc = jnp.broadcast_to(doc_in[...].astype(F32), (128 - 32, 128))
    tail = jnp.transpose(jnp.concatenate([dt_in[...].astype(F32), doc], axis=0))
    tail = tail.reshape(RUNS, RUN, 128).astype(BF16)
    pairs = bc_in[...].astype(F32)
    for k in range(2):
        for n in range(2):
            part_bc = pairs[:, n, k * 128 : k * 128 + 128].astype(BF16)
            asend[:, k, :, n * 128 : n * 128 + 128] = part_bc.reshape(RUNS, RUN, 128)
        asend[:, k, :, 256:] = tail

    pl.semaphore_wait(ready_sem, 7)

    kind = t // 63

    def x_block(b, d):
        at = pl.multiple_of((d % PIECES) * WIDTH + b * PART, 128)
        return x_hbm.at[d // PIECES, :, pl.ds(at, PART)]

    def aux_block(d):
        return asend.at[d // PIECES, (d % PIECES) // 2]

    def send_x(b, first, stop):
        @pl.loop(first, stop)
        def _(k):
            d = (role + k * 37) % HALF
            remote(
                x_block(b, d), xr.at[b, 1 + t], send_sem.at[0], recv_x.at[b, kind], half * HALF + (d ^ flip)
            ).start()

        if first == 1:
            pltpu.make_async_copy(x_block(b, role), xr.at[b, 1 + t], recv_x.at[b, kind]).start()

    @pl.loop(1, HALF // 2)
    def _(k):
        d = ((role // 2 + k * 17) % 32) * 2 + core
        remote(
            aux_block(d), ar.at[1 + chip, core], send_sem.at[1], recv_a, half * HALF + (d ^ flip)
        ).start()

    pltpu.make_async_copy(aux_block(role), ar.at[1 + chip, core], recv_a).start()
    send_x(0, 1, CUTS[0])

    z_copy.wait()
    for k in range(RUNS):
        zs[k * RUN : k * RUN + RUN] = silu(zbuf[k].astype(F32))
    send_x(0, CUTS[0], CUTS[1])

    take(ar.at[pl.ds(1, 32), core], recv_a)
    share = remote(
        ar.at[pl.ds(1, 32), core],
        ar.at[pl.ds(1, 32), core],
        share_sem.at[0],
        share_sem.at[1],
        me + 1 - 2 * core,
    )
    share.start()
    if CUTS[1] < HALF:
        send_x(0, CUTS[1], HALF)
    for b in range(1, NB):
        send_x(b, 1, HALF // 2)
    share.wait()

    following = seg_device((seg + 1) % SEGS)
    halo_a = remote(ar.at[32, 1], ar.at[0, 1], halo_a_sem.at[0], halo_a_sem.at[1], following)
    halo_a.start()

    def halo_x(b):
        return remote(
            xr.at[b, 64], xr.at[b, 0], halo_x_sem.at[b, 0], halo_x_sem.at[b, 1], following
        )

    for copy in loads[3:]:
        copy.wait()
    none = jnp.zeros((1, 96), F32)
    rates = jnp.concatenate([rate[...], none], axis=1)
    skips = jnp.concatenate([dskip[...], none], axis=1)
    lane = lax.broadcasted_iota(jnp.int32, (128, WIDTH), 1)
    row = lax.broadcasted_iota(jnp.int32, (128, WIDTH), 0)
    spread = (row == w * 8 + lax.shift_right_logical(lane, 6)).astype(F32).astype(BF16)
    spread = jnp.concatenate([spread] * 3, axis=0)

    raw = ar[1:, :, :, 256:384].astype(F32).reshape(SEG, 128)
    step = jnp.maximum(raw, 0.0) + jnp.log1p(jnp.exp(-jnp.abs(raw)))
    log_decay = split(-step * rates, 3)
    tri = (
        lax.broadcasted_iota(jnp.int32, (SPAN, SPAN), 0)
        >= lax.broadcasted_iota(jnp.int32, (SPAN, SPAN), 1)
    ).astype(F32)
    tri_bf = tri.astype(BF16)
    mids, lasts = [], []
    for c in range(2):
        at = slice(c * SPAN, c * SPAN + SPAN)
        sums = dot(tri_bf, log_decay[at])
        decay = sums[:, :128] + sums[:, 128:256] + sums[:, 256:]
        mid, end = decay[127:128], decay[255:256]
        mids.append(mid)
        lasts.append(end)
        into = jnp.exp(mid - decay) * step[at]
        xin[at] = dot(split(into, 2), spread[:256])
        eout[at] = dot(split(jnp.exp(decay - mid), 2), spread[:256])
    rows = jnp.concatenate(
        [
            jnp.exp(mids[0]),
            jnp.exp(mids[1] + lasts[0] - mids[0]),
            jnp.exp(mids[1] + lasts[0]),
            jnp.exp(lasts[0] - mids[0] + lasts[1]),
            jnp.exp(lasts[1] - mids[1]),
            skips,
            jnp.zeros((2, 128), F32),
        ],
        axis=0,
    )
    srows[...] = dot(split(rows, 3), spread)

    take(xr.at[0, pl.ds(64, 1)], recv_x.at[0, 1])
    halo_x(0).start()
    for b in range(1, NB):
        send_x(b, HALF // 2, HALF)
    halo_a.wait()

    docs = ar[:, :, :, 256:384].astype(F32).reshape(SEG + 16, 128)[8:]
    docs = jnp.broadcast_to(docs[:, 127:128], (SEG + 8, 128))
    ahead = lax.broadcasted_iota(jnp.int32, (SEG + 8, 128), 0) < 8
    docs = jnp.where(jnp.logical_and(ahead, seg == 0), -1.0, docs)
    ext[...] = docs
    own = ext[8:, :]
    for k in range(1, 4):
        same[k - 1] = (ext[8 - k : 8 - k + SEG, :] == own).astype(F32)
    before = ext[7:8, :]
    last = ext[SEG + 7 : SEG + 8, :]
    from_before = (own == before).astype(F32)
    to_last = (own == last).astype(F32)
    marks = (own == lax.broadcasted_iota(jnp.int32, (SEG, 128), 1).astype(F32)).astype(F32)
    marks = marks.astype(BF16)

    psend[...] = jnp.exp(lasts[0] + lasts[1]) * (before == last).astype(F32)

    @pl.loop(1, SEGS)
    def _(k):
        r = (seg + k * 17) % SEGS
        remote(psend, precv.at[seg], send_sem.at[5], pass_sem, seg_device(r)).start()

    pltpu.make_async_copy(psend, precv.at[seg], pass_sem).start()

    def conv(block, taps, bias):
        size = block.shape[0] - 8
        ext[: size + 8] = block
        total = bias + taps[3:4] * block[8:]
        for k in range(1, 4):
            moved = ext[8 - k : 8 - k + size, :] * same[k - 1, :size]
            total = total + taps[3 - k : 4 - k] * moved
        return silu(total).astype(BF16)

    for k in range(2):
        at = pl.ds(pl.multiple_of(group * 128, 128), 128)
        block = ar[:, :, :, k * 128 : k * 128 + 128].astype(F32)
        bcc[:, k * 128 : k * 128 + 128] = conv(
            block.reshape(SEG + 16, 128)[8:], conv_bc[:, k, at], bias_bc[k : k + 1, at]
        )
    weighted = (bcc[:, :128].astype(F32) * to_last).astype(BF16)
    reads = (bcc[:, 128:].astype(F32) * from_before).astype(BF16)

    scored = []
    for c, e in ((0, 0), (1, 1), (1, 0)):
        at, to = slice(c * SPAN, c * SPAN + SPAN), slice(e * SPAN, e * SPAN + SPAN)
        seen = dot(marks[at], marks[to], ((1,), (1,)))
        if c == e:
            seen = seen * tri
        scored.append((dot(bcc[at, 128:], bcc[to, :128], ((1,), (1,))) * seen).astype(BF16))

    for b in range(NB):
        here = slice(b * PART, b * PART + PART)
        take(xr.at[b, pl.ds(1, 63)], recv_x.at[b, 0])
        into = xin[:16, here]
        for j in range(PART // 128):
            at = slice(b * PART + j * 128, b * PART + j * 128 + 128)
            far = pl.ds(pl.multiple_of(w * WIDTH + b * PART + j * 128, 128), 128)
            block = xr[b, 1:, :, j * 128 : j * 128 + 128].astype(F32).reshape(SEG, 128)
            block = jnp.concatenate([jnp.zeros((8, 128), F32), block], axis=0)
            mixed = conv(block, conv_x[:, far], bias_x[:, far])
            xc[:, at] = mixed
            scaled = mixed.astype(F32) * xin[:, at]
            xst[:SPAN, at] = (scaled[:SPAN] * srows[3:4, at]).astype(BF16)
            xst[SPAN:, at] = (scaled[SPAN:] * srows[4:5, at]).astype(BF16)
            xin[:, at] = scaled
        if b + 1 < NB:
            take(xr.at[b + 1, pl.ds(64, 1)], recv_x.at[b + 1, 1])
            halo_x(b + 1).start()
        halo_x(b).wait()
        for j in range(PART // 128):
            at = slice(b * PART + j * 128, b * PART + j * 128 + 128)
            far = pl.ds(pl.multiple_of(w * WIDTH + b * PART + j * 128, 128), 128)
            block = xr[b, :3, :, j * 128 : j * 128 + 128].astype(F32).reshape(24, 128)
            mixed = conv(block, conv_x[:, far], bias_x[:, far])
            xc[:16, at] = mixed
            scaled = mixed.astype(F32) * into[:, j * 128 : j * 128 + 128]
            xst[:16, at] = (scaled * srows[3:4, at]).astype(BF16)
            xin[:16, at] = scaled
        state = dot(xst[:, here], weighted, ((0,), (0,)))
        sbuf[b] = state.reshape(SEGS, SLICE, 128).astype(BF16)

        @pl.loop(1, SEGS)
        def _(k):
            r = (seg + k * 17) % SEGS
            remote(
                sbuf.at[b, r], srecv.at[b, seg], send_sem.at[2], state_sem.at[b], seg_device(r)
            ).start()

        pltpu.make_async_copy(sbuf.at[b, seg], srecv.at[b, seg], state_sem.at[b]).start()

        inner[:SPAN, here] = dot(scored[0], xin[:SPAN, here].astype(BF16))
        inner[SPAN:, here] = (
            dot(scored[1], xin[SPAN:, here].astype(BF16))
            + dot(scored[2], xin[:SPAN, here].astype(BF16)) * srows[1:2, here]
        )

    take(precv, pass_sem)
    factors = precv[...].reshape(SEGS, 128)
    lanes = lax.broadcasted_iota(jnp.int32, (SEGS, 128), 1)
    for b in range(NB):
        head = lanes == w * 8 + b * (8 // NB) + seg * SLICE // HDIM
        factor = jnp.sum(jnp.where(head, factors, 0.0), axis=1, keepdims=True)
        take(srecv.at[b], state_sem.at[b])
        carried = jnp.zeros((SLICE, 128), F32)
        for g in range(SEGS):
            inb[b, g] = carried.astype(BF16)
            carried = srecv[b, g].astype(F32) + factor[g : g + 1] * carried

        @pl.loop(1, SEGS)
        def _(k):
            r = (seg + k * 17) % SEGS
            remote(
                inb.at[b, r], inr.at[b, seg], send_sem.at[3], back_sem.at[b], seg_device(r)
            ).start()

        pltpu.make_async_copy(inb.at[b, seg], inr.at[b, seg], back_sem.at[b]).start()

    for b in range(NB):
        here = slice(b * PART, b * PART + PART)
        take(inr.at[b], back_sem.at[b])
        incoming = inr[b].astype(F32).reshape(PART, 128).astype(BF16)
        for c in range(2):
            at = slice(c * SPAN, c * SPAN + SPAN)
            cross = dot(reads[at], incoming, ((1,), (1,))) * srows[2 * c : 2 * c + 1, here]
            y = (inner[at, here] + cross) * eout[at, here]
            y = y + srows[5:6, here] * xc[at, here].astype(F32)
            ysend[b, c * 32 : c * 32 + 32] = y.reshape(32, RUN, PART).astype(BF16)
        place = yrecv.at[b, q, :, pl.ds(pl.multiple_of(w * PART, 128), PART)]

        @pl.loop(1, HALF)
        def _(k):
            d = (t + k * 37) % HALF
            remote(ysend.at[b, d], place, send_sem.at[4], y_sem.at[b], half * HALF + d).start()

        pltpu.make_async_copy(ysend.at[b, t], place, y_sem.at[b]).start()

    sums = jnp.zeros((RUNS * RUN, PART), F32)
    for b in range(NB):
        take(yrecv.at[b], y_sem.at[b])
        for k in range(PIECES):
            at = slice(k * WIDTH + b * PART, k * WIDTH + b * PART + PART)
            y = yrecv[b, :, :, k * PART : k * PART + PART].astype(F32)
            gated = y.reshape(RUNS * RUN, PART) * zs[:, at]
            zs[:, at] = gated
            sums = sums + gated * gated
    square = jnp.sum(sums, axis=1, keepdims=True)
    part[col] = jnp.transpose(jnp.broadcast_to(square, (128, 128)))[:8]
    for k in range(1, n_col):
        remote(
            part.at[col], part.at[col], send_sem.at[6], part_sem, me, (col + k) % n_col
        ).start()
    take(part.at[pl.ds(0, n_col - 1)], part_sem)
    total = jnp.sum(part[...], axis=0)
    total = jnp.transpose(jnp.broadcast_to(total[:1], (128, 128)))[:, :1]
    scale = lax.rsqrt(total / DI + EPSILON)
    for k in range(LOCAL // 512):
        at = slice(k * 512, k * 512 + 512)
        out_ref[:, at] = (zs[:, at] * scale * gain[:, at]).astype(BF16)

    for b in range(NB):
        take(xr.at[b, pl.ds(0, 63)], send_sem.at[0])
        take(sbuf.at[b, pl.ds(0, 31)], send_sem.at[2])
        take(inb.at[b, pl.ds(0, 31)], send_sem.at[3])
        take(ysend.at[b, pl.ds(0, 63)], send_sem.at[4])
    take(ar.at[pl.ds(0, 31), 0], send_sem.at[1])
    take(precv.at[pl.ds(0, 31)], send_sem.at[5])
    take(part.at[pl.ds(0, n_col - 1)], send_sem.at[6])


def local(
    x_in, bc_in, dt_raw, doc_id, conv_x, bias_x, conv_bc, bias_bc, rate, dskip, z_in, norm_gain
):
    n_col = lax.axis_size("mp")
    rows = x_in.shape[0]
    heads = rate.shape[0]
    vmem = pl.BlockSpec(memory_space=pltpu.VMEM)
    hbm = pl.BlockSpec(memory_space=pltpu.HBM)
    dma = pltpu.SemaphoreType.DMA
    return pl.pallas_call(
        body,
        out_shape=jax.ShapeDtypeStruct((rows, LOCAL), BF16),
        in_specs=[hbm] * 12,
        out_specs=vmem,
        scratch_shapes=[
            pltpu.VMEM((rows, 2, 256), BF16),
            pltpu.VMEM((heads, rows), BF16),
            pltpu.VMEM((1, rows), jnp.int32),
            pltpu.VMEM((4, LOCAL), F32),
            pltpu.VMEM((1, LOCAL), F32),
            pltpu.VMEM((4, 2, 256), F32),
            pltpu.VMEM((2, 256), F32),
            pltpu.VMEM((1, heads), F32),
            pltpu.VMEM((1, heads), F32),
            pltpu.VMEM((1, LOCAL), F32),
            pltpu.VMEM((RUNS, 2, RUN, AUX), BF16),
            pltpu.VMEM((NB, 65, RUN, PART), BF16),
            pltpu.VMEM((33, 2, RUN, AUX), BF16),
            pltpu.VMEM((SEG + 8, 128), F32),
            pltpu.VMEM((3, SEG, 128), F32),
            pltpu.VMEM((SEG, WIDTH), BF16),
            pltpu.VMEM((SEG, 256), BF16),
            pltpu.VMEM((SEG, WIDTH), F32),
            pltpu.VMEM((SEG, WIDTH), BF16),
            pltpu.VMEM((SEG, WIDTH), F32),
            pltpu.VMEM((SEG, WIDTH), F32),
            pltpu.VMEM((8, WIDTH), F32),
            pltpu.VMEM((1, 128), F32),
            pltpu.VMEM((SEGS, 1, 128), F32),
            pltpu.VMEM((NB, SEGS, SLICE, 128), BF16),
            pltpu.VMEM((NB, SEGS, SLICE, 128), BF16),
            pltpu.VMEM((NB, SEGS, SLICE, 128), BF16),
            pltpu.VMEM((NB, SEGS, SLICE, 128), BF16),
            pltpu.VMEM((NB, 64, RUN, PART), BF16),
            pltpu.VMEM((NB, RUNS, RUN, PIECES * PART), BF16),
            pltpu.VMEM((RUNS, RUN, LOCAL), BF16),
            pltpu.VMEM((RUNS * RUN, LOCAL), F32),
            pltpu.VMEM((n_col, 8, 128), F32),
            pltpu.SemaphoreType.REGULAR,
            dma((7,)),
            dma((NB, 2)),
            dma,
            dma((2,)),
            dma((NB, 2)),
            dma((2,)),
            dma,
            dma((NB,)),
            dma((NB,)),
            dma((NB,)),
            dma,
            dma,
            dma((10,)),
        ],
        compiler_params=pltpu.CompilerParams(
            collective_id=0, has_side_effects=True, vmem_limit_bytes=60 * 2**20
        ),
    )(
        x_in.reshape(RUNS, RUN, LOCAL),
        z_in.reshape(RUNS, RUN, LOCAL),
        bc_in,
        dt_raw.T,
        doc_id[None],
        conv_x,
        bias_x[None],
        conv_bc,
        bias_bc,
        rate[None],
        dskip[None],
        norm_gain[None],
    )


def solution(mesh):
    placed = (
        P("seq", "mp"),
        P("seq", None, "mp"),
        P("seq", "mp"),
        P("seq"),
        P(None, "mp"),
        P("mp"),
        P(None, None, "mp"),
        P(None, "mp"),
        P("mp"),
        P("mp"),
        P("seq", "mp"),
        P("mp"),
    )
    return jax.shard_map(
        local, mesh=mesh, in_specs=placed, out_specs=P("seq", "mp"), check_vma=False
    )
```
